32 devices in a mesh: member: 2 (over x), grid: 16 (over z, y, core).
Axes of the slice: x: 2, y: 2, z: 4, core: 2. Of those that a mesh axis runs over, the one named last changes fastest.
Arguments:
- states: bfloat16 [2, 2048, 1024], P('member', 'grid'), may hold values from -6 to 6
- norm_scale_vector: float32 [1024], replicated, may hold values from 0.1 to 1.9
- query_weight: bfloat16 [1024, 512], P('grid'), may hold values from -2 to 2
- key_weight: bfloat16 [1024, 512], P('grid'), may hold values from -2 to 2
- value_weight: bfloat16 [1024, 512], P('grid'), may hold values from -0.1875 to 0.1875
- output_weight: bfloat16 [512, 1024], P('grid'), may hold values from -0.25 to 0.25
- head_weight: bfloat16 [1024, 128], P('grid'), may hold values from -0.5 to 0.5
- neighbours: int32 [2048, 8], P('grid'), may hold values from 0 to 2047, as said below
- observed: float32 [2048, 128], P('grid'), may hold values from -16 to 16
Outputs:
- grad_input: bfloat16 [2, 2048, 1024], P('member', 'grid')
- grad_mixing: float32 [512, 1024], P('grid')
- grad_head: float32 [1024, 128], P('grid')
- grad_key_value: float32 [2, 2048, 1024], P('member', 'grid')
The draws below stay inside these ranges and needn't reach their ends.
Inputs may be any that keep to these rules, and one draw needn't show every extreme that they name: `neighbours`: the first neighbour of every point is the point itself; every neighbour index lies within 32 positions of the point's own index, and that distance occurs.
All inputs are finite; a program needn't handle non-finite values.
Results may differ from the reference program's by a relative error of at most 0.035.
Values may be sent and summed in bfloat16 or wider, within the bound.
A program may use at most 64 MiB of HBM per device.

```python
import math
import jax
import jax.numpy as jnp
from jax import lax

D = 1024
HEADS = 8
HDIM = 64
NVAR = 128
KNB = 8
P_DEV = 128
HD = 512
HALO = 32
NPTS = 2048
ENSEMBLE_SIZE = 2
N_GRID = 16


def query_and_key(key):
    base_draw = jnp.clip(jax.random.normal(jax.random.fold_in(key, 101), (D, HD), jnp.float32), -6.0, 6.0)
    w_first = base_draw * D ** (-0.5)
    jitter = jnp.clip(jax.random.normal(jax.random.fold_in(key, 102), (D, HD), jnp.float32), -6.0, 6.0) * D ** (-0.5)
    w_second = jitter
    return (jnp.clip(w_first, -2.0, 2.0), w_second)


def draw_query_weight(key, part):
    return query_and_key(key)[0].astype(jnp.bfloat16)


def draw_key_weight(key, part):
    return query_and_key(key)[1].astype(jnp.bfloat16)


def draw_neighbours(key, part):
    offsets = jax.random.randint(jax.random.fold_in(key, 201), (NPTS, KNB), -HALO, HALO + 1, dtype=jnp.int32)
    offsets = offsets.at[:, 0].set(0)
    offsets = offsets.at[HALO, 1].set(-HALO)
    offsets = offsets.at[NPTS - 1 - HALO, 1].set(HALO)
    position = jnp.arange(NPTS, dtype=jnp.int32)[:, None]
    return jnp.clip(position + offsets, 0, NPTS - 1).astype(jnp.int32)


def with_spikes(array, stream_key, source, target, shards_of, factor):
    owner, partner = [(jnp.arange(array.shape[dim]) // (array.shape[dim] // shards_of)).reshape([-1 if axis == dim else 1 for axis in range(array.ndim)]) for dim in (source, target)]
    chosen = jax.random.permutation(stream_key, shards_of)[partner]
    strong = (owner == chosen) | (owner == (partner + shards_of // 2) % shards_of)
    return jnp.where(strong, factor * array, array)


def levels(stream_key, extent, cuts, least, largest):
    level = 1.0
    for dim, parts in cuts:
        heights = jax.random.uniform(jax.random.fold_in(jax.random.fold_in(stream_key, 6), dim), (parts,), jnp.float32, least / len(cuts), largest / len(cuts))
        level = level * jnp.repeat(jnp.exp(heights), extent[dim] // parts).reshape((-1,) + (1,) * (len(extent) - 1 - dim))
    return level


def bell_draw(key, shape, scale, limit, shards=(), held_as=jnp.bfloat16):
    drawn = jax.random.normal(key, shape, jnp.float32) * scale
    if len(shards) > 0:
        drawn = levels(key, shape, shards, -0.22, 0.18) * drawn
    return jnp.clip(drawn, min=-limit, max=limit).astype(held_as)


def noise_with(key, extent, scale, bound, cuts, heavy, kind=jnp.bfloat16):
    array = scale * jax.random.normal(key, extent, jnp.float32)
    if cuts:
        array = array * levels(key, extent, cuts, -0.22, 0.18)
    return jnp.clip(with_spikes(array, jax.random.fold_in(key, 3), *heavy), -bound, bound).astype(kind)


def setup_inputs(seed: int = 0) -> dict:
    keys = jax.random.split(jax.random.key(seed), 10)
    return {
        "states": noise_with(keys[0], (ENSEMBLE_SIZE, NPTS, D), 1.0, 6.0, ((0, 2), (1, 16)), (1, 2, 16, 2.0)),
        "norm_scale_vector": jnp.clip(1.0 + 0.18 * jax.random.normal(keys[1], (D,), jnp.float32), 0.1, 1.9),
        "query_weight": draw_query_weight(jax.random.fold_in(keys[9], 71), 0),
        "key_weight": draw_key_weight(jax.random.fold_in(keys[9], 71), 0),
        "value_weight": bell_draw(keys[4], (D, HD), D ** -0.5, 0.1875, ((0, 16),)),
        "output_weight": bell_draw(keys[5], (HD, D), HD ** -0.5, 0.25, ((0, 16),)),
        "head_weight": bell_draw(keys[6], (D, NVAR), NVAR ** -0.5, 0.5, ((0, 16),)),
        "neighbours": draw_neighbours(jax.random.fold_in(keys[9], 71), 0),
        "observed": bell_draw(keys[8], (NPTS, NVAR), 3.0, 16.0, ((0, 16),), jnp.float32),
    }


epsilon = 1e-05
smooth = 0.1

def layer_norm(states, norm_scale_vector):
    values = states.astype(jnp.float32)
    center = values - lax.optimization_barrier(jnp.mean(values, axis=-1, keepdims=True))
    inverse_spread = lax.rsqrt(lax.optimization_barrier(jnp.mean(center * center, axis=-1, keepdims=True)) + epsilon)
    return (center * inverse_spread, inverse_spread)

def gradient_of(spread):
    return spread / jnp.sqrt(spread * spread + smooth * smooth)

def attend(query_rows, gathered):
    number = query_rows.shape[0]
    query_heads = query_rows.astype(jnp.float32).reshape(number, HEADS, HDIM)
    key_heads = gathered[:, :, :HD].astype(jnp.float32).reshape(number, KNB, HEADS, HDIM)
    value_heads = gathered[:, :, HD:].astype(jnp.float32).reshape(number, KNB, HEADS, HDIM)
    scores = jnp.einsum('rhe,rkhe->rhk', query_heads, key_heads) * (1.0 / math.sqrt(HDIM))
    highest = lax.optimization_barrier(jnp.max(scores, axis=-1, keepdims=True))
    exponent = jnp.exp(scores - highest)
    attention = exponent / lax.optimization_barrier(jnp.sum(exponent, axis=-1, keepdims=True))
    attention_cast = attention.astype(jnp.bfloat16)
    attended_rows = jnp.einsum('rhk,rkhe->rhe', attention_cast.astype(jnp.float32), value_heads)
    return (attended_rows.reshape(number, HD).astype(jnp.bfloat16), attention, attention_cast)

def attend_back(query_rows, gathered, attention, attention_cast, grad_mixed):
    number = query_rows.shape[0]
    query_heads = query_rows.astype(jnp.float32).reshape(number, HEADS, HDIM)
    key_heads = gathered[:, :, :HD].astype(jnp.float32).reshape(number, KNB, HEADS, HDIM)
    value_heads = gathered[:, :, HD:].astype(jnp.float32).reshape(number, KNB, HEADS, HDIM)
    grad_heads = grad_mixed.astype(jnp.float32).reshape(number, HEADS, HDIM)
    grad_prob = jnp.einsum('rhe,rkhe->rhk', grad_heads, value_heads)
    grad_score = attention * (grad_prob - lax.optimization_barrier(jnp.sum(attention * grad_prob, axis=-1, keepdims=True))) * (1.0 / math.sqrt(HDIM))
    grad_query = jnp.einsum('rhk,rkhe->rhe', grad_score, key_heads)
    grad_keys = jnp.einsum('rhk,rhe->rkhe', grad_score, query_heads)
    grad_values = jnp.einsum('rhk,rhe->rkhe', attention_cast.astype(jnp.float32), grad_heads)
    returned = jnp.concatenate([grad_keys.reshape(number, KNB, HD), grad_values.reshape(number, KNB, HD)], axis=-1)
    return (grad_query.reshape(number, HD).astype(jnp.bfloat16), returned)

def forward_pass(states, norm_scale_vector, query_weight, key_weight, value_weight, output_weight, head_weight, neighbours):
    centred_rows, inverse_spread = layer_norm(states, norm_scale_vector)
    normed = (centred_rows * norm_scale_vector).astype(jnp.bfloat16)
    query_rows = jnp.dot(normed, query_weight, preferred_element_type=jnp.float32).astype(jnp.bfloat16)
    key_part = jnp.dot(normed, key_weight, preferred_element_type=jnp.float32).astype(jnp.bfloat16)
    value_part = jnp.dot(normed, value_weight, preferred_element_type=jnp.float32).astype(jnp.bfloat16)
    key_value_pair = jnp.concatenate([key_part, value_part], axis=1)

    def one_block(pair_rows):
        row_block, nearby = pair_rows
        mixed_rows, attention, attention_cast = attend(row_block, jnp.take(key_value_pair, nearby, axis=0))
        return mixed_rows
    attended_rows = lax.map(one_block, (query_rows.reshape(N_GRID, P_DEV, HD), neighbours.reshape(N_GRID, P_DEV, KNB))).reshape(NPTS, HD)
    layer_output = (states.astype(jnp.float32) + jnp.dot(attended_rows, output_weight, preferred_element_type=jnp.float32)).astype(jnp.bfloat16)
    member_prediction = jnp.dot(layer_output, head_weight, preferred_element_type=jnp.float32)
    return (centred_rows, inverse_spread, query_rows, key_value_pair, attended_rows, layer_output, member_prediction)

def reference(states, norm_scale_vector, query_weight, key_weight, value_weight, output_weight, head_weight, neighbours, observed):

    def prediction_only(ensemble_states):
        return forward_pass(ensemble_states, norm_scale_vector, query_weight, key_weight, value_weight, output_weight, head_weight, neighbours)[6]
    ensemble_predictions = lax.map(prediction_only, states)
    pairwise_total = jnp.zeros_like(ensemble_predictions)
    for member_index in range(ENSEMBLE_SIZE):
        pairwise_total = pairwise_total + gradient_of(ensemble_predictions - ensemble_predictions[member_index][None])
    prediction_gradient = (gradient_of(ensemble_predictions - observed[None]) - pairwise_total / (ENSEMBLE_SIZE - 1)).astype(jnp.bfloat16)

    def member_step(totals, item):
        ensemble_states, member_grad = item
        centred_rows, inverse_spread, query_rows, key_value_pair, attended_rows, layer_output, member_prediction = forward_pass(ensemble_states, norm_scale_vector, query_weight, key_weight, value_weight, output_weight, head_weight, neighbours)
        grad_output = jnp.dot(member_grad, head_weight.T, preferred_element_type=jnp.float32)
        output_cast = grad_output.astype(jnp.bfloat16)
        grad_mixed = jnp.dot(output_cast, output_weight.T, preferred_element_type=jnp.float32).astype(jnp.bfloat16)
        mixing_total = totals[0] + jnp.dot(attended_rows.astype(jnp.float32).T, grad_output, precision=lax.Precision.HIGHEST)
        head_total = totals[1] + jnp.dot(layer_output.T, member_grad, preferred_element_type=jnp.float32)

        def block_back(accumulated, triple):
            row_block, nearby, grad_rows = triple
            gathered = jnp.take(key_value_pair, nearby, axis=0)
            mixed_rows, attention, attention_cast = attend(row_block, gathered)
            grad_query, returned = attend_back(row_block, gathered, attention, attention_cast, grad_rows)
            accumulated = accumulated.at[nearby.reshape(-1)].add(returned.reshape(-1, 2 * HD))
            return (accumulated, grad_query)
        accumulated, grad_query = lax.scan(block_back, jnp.zeros((NPTS, 2 * HD), jnp.float32), (query_rows.reshape(N_GRID, P_DEV, HD), neighbours.reshape(N_GRID, P_DEV, KNB), grad_mixed.reshape(N_GRID, P_DEV, HD)))
        grad_query = grad_query.reshape(NPTS, HD)
        grad_keys = accumulated[:, :HD].astype(jnp.bfloat16)
        grad_values = accumulated[:, HD:].astype(jnp.bfloat16)
        grad_normed = jnp.dot(grad_query, query_weight.T, preferred_element_type=jnp.float32)
        grad_normed = grad_normed + jnp.dot(grad_keys, key_weight.T, preferred_element_type=jnp.float32)
        grad_normed = grad_normed + jnp.dot(grad_values, value_weight.T, preferred_element_type=jnp.float32)
        grad_centred = grad_normed * norm_scale_vector
        grad_states = inverse_spread * (grad_centred - lax.optimization_barrier(jnp.mean(grad_centred, axis=-1, keepdims=True)) - centred_rows * lax.optimization_barrier(jnp.mean(grad_centred * centred_rows, axis=-1, keepdims=True)))
        return ((mixing_total, head_total), ((grad_output + grad_states).astype(jnp.bfloat16), accumulated))
    starting = (jnp.zeros((HD, D), jnp.float32), jnp.zeros((D, NVAR), jnp.float32))
    totals, member_outputs = lax.scan(member_step, starting, (states, prediction_gradient))
    grad_input, grad_key_value = member_outputs
    scaling = 1.0 / math.sqrt(ENSEMBLE_SIZE * NPTS)
    return (grad_input, totals[0] * scaling, totals[1] * scaling, grad_key_value)
```

```python
import functools
import math

import jax
import jax.numpy as jnp
from jax import lax
from jax.experimental import pallas as pl
from jax.experimental.pallas import tpu as pltpu
from jax.sharding import PartitionSpec as P

HEADS = 8
HALO = 32
MESH = pl.DeviceIdType.MESH

epsilon = 1e-05
smooth = 0.1

BF = jnp.bfloat16
F32 = jnp.float32


def dot(left, right, left_dim=1, right_dim=0):
    return lax.dot_general(
        left,
        right,
        (((left_dim,), (right_dim,)), ((), ())),
        preferred_element_type=F32,
    )


def gradient_of(spread):
    return spread * lax.rsqrt(spread * spread + smooth * smooth)


def factors(total):
    pair = 2 if total % 2 == 0 else 1
    near = 2 if (total // pair) % 2 == 0 else 1
    return total // (pair * near), near, pair


def kernel(
    members,
    grid,
    states,
    gain,
    wq,
    wk,
    wv,
    wo,
    wh,
    nb,
    obs,
    grad_input,
    grad_mixing,
    grad_head,
    grad_kv,
    qkv_all,
    wo_all,
    wh_all,
    centred,
    normed,
    query,
    ext,
    att,
    prob,
    mixed,
    layer_out,
    forecasts,
    grad_out,
    grad_mixed,
    grad_query,
    grad_ext,
    halo_out,
    halo_in,
    stage,
    shares,
    gather_send,
    gather_recv,
    halo_send,
    halo_recv,
    fore_send,
    fore_recv,
    share_send,
    share_recv,
):
    everyone = members * grid
    m = lax.axis_index("member")
    g = lax.axis_index("grid")
    me = m * grid + g
    points, width = states.shape[1], states.shape[2]
    inner = wq.shape[1]
    extent = points + 2 * HALO
    variables = obs.shape[1]
    head_dim = inner // HEADS
    far, near, pair = factors(grid)
    a, b, c = g // (near * pair), (g // pair) % near, g % pair

    def remote(src, dst, send, recv, mt, gt):
        return pltpu.make_async_remote_copy(
            src_ref=src,
            dst_ref=dst,
            send_sem=send,
            recv_sem=recv,
            device_id={"member": mt, "grid": gt},
            device_id_type=MESH,
        )

    barrier = pltpu.get_barrier_semaphore()

    def greet(i, carry):
        t = lax.rem(me + i, everyone)
        pl.semaphore_signal(
            barrier,
            inc=1,
            device_id={"member": t // grid, "grid": lax.rem(t, grid)},
            device_id_type=MESH,
        )
        return carry

    lax.fori_loop(1, everyone, greet, 0)

    qkv_all[g, :, 0:inner] = wq[...]
    qkv_all[g, :, inner : 2 * inner] = wk[...]
    qkv_all[g, :, 2 * inner : 3 * inner] = wv[...]
    wo_all[g] = wo[...]
    wh_all[g] = wh[...]
    pl.semaphore_wait(barrier, everyone - 1)

    pending = []

    def at(ai, bi, ci):
        return (ai * near + bi) * pair + ci

    def gather(buffers, base):
        counter = [0]

        def send(slot, gt):
            for n, buf in enumerate(buffers):
                copy = remote(
                    buf.at[slot],
                    buf.at[slot],
                    gather_send.at[base + n, counter[0]],
                    gather_recv.at[base + n, slot],
                    m,
                    gt,
                )
                copy.start()
                pending.append(copy)
            counter[0] += 1

        def arrived(slot):
            for n, buf in enumerate(buffers):
                remote(
                    buf.at[slot],
                    buf.at[slot],
                    gather_send.at[base + n, 0],
                    gather_recv.at[base + n, slot],
                    m,
                    g,
                ).wait_recv()

        other_b = lax.rem(b + 1, near)
        other_c = lax.rem(c + 1, pair)

        def begin():
            for i in range(1, far):
                send(g, at(lax.rem(a + i, far), b, c))
            if near > 1:
                send(g, at(a, other_b, c))
            if pair > 1:
                send(g, at(a, b, other_c))

        def from_far(i):
            slot = at(lax.rem(a + i, far), b, c)
            arrived(slot)
            if near > 1:
                send(slot, at(a, other_b, c))
            if pair > 1:
                send(slot, at(a, b, other_c))

        def from_near(i):
            slot = at(lax.rem(a + i, far), other_b, c)
            arrived(slot)
            if pair > 1:
                send(slot, at(a, b, other_c))

        steps = []
        for i in range(1, far):
            steps.append(functools.partial(from_far, i))
            if near > 1:
                steps.append(functools.partial(from_near, i - 1))
        if near > 1:
            steps.append(functools.partial(from_near, far - 1))

        def finish():
            if pair > 1:
                for i in range(far):
                    for j in range(near):
                        arrived(at(lax.rem(a + i, far), lax.rem(b + j, near), other_c))

        return begin, steps, finish

    begin_qkv, steps_qkv, finish_qkv = gather([qkv_all], 0)
    begin_out, steps_out, finish_out = gather([wo_all, wh_all], 1)

    begin_qkv()

    x = states[0].astype(F32)
    center = x - jnp.mean(x, axis=-1, keepdims=True)
    inverse = lax.rsqrt(jnp.mean(center * center, axis=-1, keepdims=True) + epsilon)
    centred[...] = center * inverse
    normed[...] = (centred[...] * gain[...]).astype(BF)

    local = nb[...] - (g * points - HALO)
    column = lax.broadcasted_iota(jnp.int32, (points, extent), 1)
    count = jnp.zeros((points, extent), F32)
    for k in range(nb.shape[1]):
        count = count + (local[:, k : k + 1] == column).astype(F32)
    count2 = jnp.concatenate([count, count], axis=0)

    for step in steps_qkv:
        step()
    begin_out()
    finish_qkv()

    kv = dot(normed[...], qkv_all[:, :, inner : 3 * inner].reshape(width, 2 * inner))
    ext[HALO : HALO + points, :] = kv.astype(BF)
    after, before = lax.rem(g + 1, grid), lax.rem(g + grid - 1, grid)
    up = remote(
        ext.at[pl.ds(points, HALO)],
        ext.at[pl.ds(0, HALO)],
        halo_send.at[0],
        halo_recv.at[0],
        m,
        after,
    )
    down = remote(
        ext.at[pl.ds(HALO, HALO)],
        ext.at[pl.ds(points + HALO, HALO)],
        halo_send.at[1],
        halo_recv.at[1],
        m,
        before,
    )
    up.start()
    down.start()
    query[...] = dot(
        normed[...], qkv_all[:, :, 0:inner].reshape(width, inner)
    ).astype(BF)
    up.wait()
    down.wait()

    lanes = 2 * head_dim
    first = lax.broadcasted_iota(jnp.int32, (points, lanes), 1) < head_dim
    scale = 1.0 / math.sqrt(head_dim)

    def stacked(rows):
        zero = jnp.zeros_like(rows)
        return jnp.concatenate(
            [jnp.where(first, rows, zero), jnp.where(first, zero, rows)], axis=0
        )

    def merged(rows):
        return jnp.where(first, rows[:points], rows[points:])

    couples = HEADS // 2
    per = -(-len(steps_out) // couples)
    for p in range(couples):
        cols = slice(p * lanes, (p + 1) * lanes)
        vcols = slice(inner + p * lanes, inner + (p + 1) * lanes)
        q2 = stacked(query[:, cols])
        score = dot(q2, ext[:, cols], 1, 1) * scale
        score = jnp.where(count2 > 0, score, -1e30)
        highest = jnp.max(score, axis=-1, keepdims=True)
        e = jnp.exp(score - highest)
        attention = e / jnp.sum(e * count2, axis=-1, keepdims=True)
        att[p] = attention
        weight = (attention.astype(BF).astype(F32) * count2).astype(BF)
        prob[p] = weight
        mixed[:, cols] = merged(dot(weight, ext[:, vcols])).astype(BF)
        for step in steps_out[p * per : (p + 1) * per]:
            step()
    finish_out()

    out_full = wo_all[...].reshape(inner, width)
    head_full = wh_all[...].reshape(width, variables)
    layer_out[...] = (states[0].astype(F32) + dot(mixed[...], out_full)).astype(BF)
    forecasts[m] = dot(layer_out[...], head_full)
    fore = []
    for i in range(1, members):
        copy = remote(
            forecasts.at[m],
            forecasts.at[m],
            fore_send.at[i],
            fore_recv.at[m],
            lax.rem(m + i, members),
            g,
        )
        copy.start()
        fore.append(copy)
    mine = forecasts[m]
    slope = gradient_of(mine - obs[...])
    for i in range(1, members):
        j = lax.rem(m + i, members)
        remote(
            forecasts.at[j], forecasts.at[j], fore_send.at[i], fore_recv.at[j], m, g
        ).wait_recv()
        slope = slope - gradient_of(mine - forecasts[j]) / (members - 1)
    grad_fore = slope.astype(BF)

    rows_head, rows_mix = wh.shape[0], wo.shape[0]
    stage[:, 0:rows_head, :] = (
        dot(layer_out[...], grad_fore, 0, 0)
        .astype(BF)
        .reshape(grid, rows_head, variables)
    )
    stage[:, rows_head : rows_head + rows_mix, :] = (
        dot(mixed[...], grad_fore, 0, 0).astype(BF).reshape(grid, rows_mix, variables)
    )

    def share(i):
        t = lax.rem(me + i, everyone)
        gt = lax.rem(t, grid)
        return remote(
            stage.at[gt],
            shares.at[me],
            share_send.at[i],
            share_recv.at[me],
            t // grid,
            gt,
        )

    def share_start(i, carry):
        share(i).start()
        return carry

    lax.fori_loop(1, everyone, share_start, 0)

    grad_out[...] = dot(grad_fore, head_full, 1, 1)
    grad_mixed[...] = dot(grad_out[...].astype(BF), out_full, 1, 1).astype(BF)

    for p in range(couples):
        cols = slice(p * lanes, (p + 1) * lanes)
        vcols = slice(inner + p * lanes, inner + (p + 1) * lanes)
        q2 = stacked(query[:, cols])
        g2 = stacked(grad_mixed[:, cols])
        attention = att[p]
        grad_prob = dot(g2, ext[:, vcols], 1, 1)
        weighted = attention * count2
        middle = jnp.sum(weighted * grad_prob, axis=-1, keepdims=True)
        grad_score = (weighted * (grad_prob - middle) * scale).astype(BF)
        grad_ext[:, cols] = dot(grad_score, q2, 0, 0)
        grad_ext[:, vcols] = dot(prob[p], g2, 0, 0)
        grad_query[:, cols] = merged(dot(grad_score, ext[:, cols])).astype(BF)

    halo_out[0] = grad_ext[0:HALO, :].astype(BF)
    halo_out[1] = grad_ext[points + HALO : points + 2 * HALO, :].astype(BF)
    back_down = remote(
        halo_out.at[0], halo_in.at[0], halo_send.at[2], halo_recv.at[2], m, before
    )
    back_up = remote(
        halo_out.at[1], halo_in.at[1], halo_send.at[3], halo_recv.at[3], m, after
    )
    back_down.start()
    back_up.start()
    grad_normed = dot(
        grad_query[...], qkv_all[:, :, 0:inner].reshape(width, inner), 1, 1
    )
    back_down.wait()
    back_up.wait()
    grad_kv[0] = grad_ext[HALO : HALO + points, :]
    grad_kv[0, 0:HALO, :] += halo_in[1].astype(F32)
    grad_kv[0, points - HALO : points, :] += halo_in[0].astype(F32)
    grad_normed = grad_normed + dot(
        grad_kv[0].astype(BF),
        qkv_all[:, :, inner : 3 * inner].reshape(width, 2 * inner),
        1,
        1,
    )
    gg = grad_normed * gain[...]
    cen = centred[...]
    grad_states = inverse * (
        gg
        - jnp.mean(gg, axis=-1, keepdims=True)
        - cen * jnp.mean(gg * cen, axis=-1, keepdims=True)
    )
    grad_input[0] = (grad_out[...] + grad_states).astype(BF)

    def share_sum(i, total):
        s = lax.rem(me + everyone - i, everyone)
        remote(
            stage.at[g], shares.at[s], share_send.at[i], share_recv.at[s], m, g
        ).wait_recv()
        return total + shares[s].astype(F32)

    total = lax.fori_loop(1, everyone, share_sum, stage[g].astype(F32))
    scaling = 1.0 / math.sqrt(members * grid * points)
    grad_head[...] = total[0:rows_head] * scaling
    grad_mixing[...] = (
        dot(total[rows_head : rows_head + rows_mix].astype(BF), head_full, 1, 1)
        * scaling
    )

    def share_done(i, carry):
        share(i).wait_send()
        return carry

    lax.fori_loop(1, everyone, share_done, 0)
    for copy in pending:
        copy.wait_send()
    for copy in fore:
        copy.wait_send()


def solution(mesh):
    members, grid = mesh.shape["member"], mesh.shape["grid"]
    far, near, pair = factors(grid)

    def shards(states, gain, wq, wk, wv, wo, wh, nb, obs):
        points, width = states.shape[1], states.shape[2]
        inner = wq.shape[1]
        variables = obs.shape[1]
        extent = points + 2 * HALO
        everyone = members * grid
        slab = wh.shape[0] + wo.shape[0]
        sends = grid
        vm = pltpu.VMEM
        dma = pltpu.SemaphoreType.DMA
        couples = HEADS // 2
        return pl.pallas_call(
            functools.partial(kernel, members, grid),
            out_shape=(
                jax.ShapeDtypeStruct((1, points, width), BF),
                jax.ShapeDtypeStruct(wo.shape, F32),
                jax.ShapeDtypeStruct(wh.shape, F32),
                jax.ShapeDtypeStruct((1, points, 2 * inner), F32),
            ),
            in_specs=[pl.BlockSpec(memory_space=pltpu.VMEM)] * 9,
            out_specs=(pl.BlockSpec(memory_space=pltpu.VMEM),) * 4,
            scratch_shapes=[
                vm((grid, wq.shape[0], 3 * inner), BF),
                vm((grid,) + wo.shape, BF),
                vm((grid,) + wh.shape, BF),
                vm((points, width), F32),
                vm((points, width), BF),
                vm((points, inner), BF),
                vm((extent, 2 * inner), BF),
                vm((couples, 2 * points, extent), F32),
                vm((couples, 2 * points, extent), BF),
                vm((points, inner), BF),
                vm((points, width), BF),
                vm((members, points, variables), F32),
                vm((points, width), F32),
                vm((points, inner), BF),
                vm((points, inner), BF),
                vm((extent, 2 * inner), F32),
                vm((2, HALO, 2 * inner), BF),
                vm((2, HALO, 2 * inner), BF),
                vm((grid, slab, variables), BF),
                vm((everyone, slab, variables), BF),
                dma((3, sends)),
                dma((3, grid)),
                dma((4,)),
                dma((4,)),
                dma((members,)),
                dma((members,)),
                dma((everyone,)),
                dma((everyone,)),
            ],
            compiler_params=pltpu.CompilerParams(
                collective_id=0,
                has_side_effects=True,
                vmem_limit_bytes=44 * 1024 * 1024,
            ),
        )(states, gain.reshape(1, width), wq, wk, wv, wo, wh, nb, obs)

    return jax.shard_map(
        shards,
        mesh=mesh,
        in_specs=(
            P("member", "grid", None),
            P(),
            P("grid", None),
            P("grid", None),
            P("grid", None),
            P("grid", None),
            P("grid", None),
            P("grid", None),
            P("grid", None),
        ),
        out_specs=(
            P("member", "grid", None),
            P("grid", None),
            P("grid", None),
            P("member", "grid", None),
        ),
        check_vma=False,
    )
```

```python
import functools
import math

import jax
import jax.numpy as jnp
from jax import lax
from jax.experimental import pallas as pl
from jax.experimental.pallas import tpu as pltpu
from jax.sharding import PartitionSpec as P

HEADS = 8
HALO = 32
MESH = pl.DeviceIdType.MESH

epsilon = 1e-05
smooth = 0.1

BF = jnp.bfloat16
F32 = jnp.float32


def dot(left, right, left_dim=1, right_dim=0):
    return lax.dot_general(
        left,
        right,
        (((left_dim,), (right_dim,)), ((), ())),
        preferred_element_type=F32,
    )


def gradient_of(spread):
    return spread * lax.rsqrt(spread * spread + smooth * smooth)


def factors(total):
    pair = 2 if total % 2 == 0 else 1
    near = 2 if (total // pair) % 2 == 0 else 1
    return total // (pair * near), near, pair


def kernel(
    members,
    grid,
    states_hbm,
    gain_hbm,
    wq,
    wk,
    wv,
    wo,
    wh,
    nb_hbm,
    obs_hbm,
    grad_input,
    grad_mixing,
    grad_head,
    grad_kv,
    states,
    gain,
    nb,
    obs,
    qkv_all,
    wo_all,
    wh_all,
    centred,
    normed,
    query,
    ext,
    att,
    prob,
    mixed,
    layer_out,
    forecasts,
    grad_out,
    grad_mixed,
    grad_query,
    grad_ext,
    halo_out,
    halo_in,
    stage,
    sibling,
    stage_sum,
    shares,
    totals,
    load_sem,
    gather_send,
    gather_recv,
    halo_send,
    halo_recv,
    fore_send,
    fore_recv,
    share_send,
    share_recv,
    total_send,
    total_recv,
):
    m = lax.axis_index("member")
    g = lax.axis_index("grid")
    points, width = states.shape[1], states.shape[2]
    inner = wq.shape[1]
    extent = points + 2 * HALO
    variables = obs.shape[1]
    head_dim = inner // HEADS
    far, near, pair = factors(grid)
    a, b, c = g // (near * pair), (g // pair) % near, g % pair
    quads, quad = grid // pair, g // pair
    after, before = lax.rem(g + 1, grid), lax.rem(g + grid - 1, grid)

    def remote(src, dst, send, recv, mt, gt):
        return pltpu.make_async_remote_copy(
            src_ref=src,
            dst_ref=dst,
            send_sem=send,
            recv_sem=recv,
            device_id={"member": mt, "grid": gt},
            device_id_type=MESH,
        )

    loads = [
        pltpu.make_async_copy(src, dst, load_sem.at[n])
        for n, (src, dst) in enumerate(
            [
                (wq, qkv_all.at[g, :, pl.ds(0, inner)]),
                (wk, qkv_all.at[g, :, pl.ds(inner, inner)]),
                (wv, qkv_all.at[g, :, pl.ds(2 * inner, inner)]),
                (states_hbm, states),
                (gain_hbm, gain),
                (nb_hbm, nb),
                (wo, wo_all.at[g]),
                (wh, wh_all.at[g]),
                (obs_hbm, obs),
            ]
        )
    ]
    for load in loads:
        load.start()

    barrier = pltpu.get_barrier_semaphore()
    peers = [(m, after), (m, before)]
    peers += [(m, lax.rem(quad + i, quads) * pair + c) for i in range(1, quads)]
    peers += [(m, quad * pair + lax.rem(c + i, pair)) for i in range(1, pair)]
    peers += [(lax.rem(m + i, members), g) for i in range(1, members)]
    for mt, gt in peers:
        pl.semaphore_signal(
            barrier, inc=1, device_id={"member": mt, "grid": gt}, device_id_type=MESH
        )
    for load in loads[:3]:
        load.wait()
    pl.semaphore_wait(barrier, len(peers))

    pending = []

    def at(ai, bi, ci):
        return (ai * near + bi) * pair + ci

    def along(i):
        if i == 0:
            return a
        if far != 4:
            return lax.rem(a + i, far)
        if i == 1:
            return a + 1 - 2 * lax.rem(a, 2)
        if i == 2:
            return lax.rem(a + 2, 4)
        return 3 - a

    other_m, other_b, other_c = 1 - m, lax.rem(b + 1, near), lax.rem(c + 1, pair)
    line = [2, 1, 3] if far == 4 else list(range(1, far))

    def gather(buf, base, split):
        counter = [0]
        quarter = buf.shape[2] // 4

        def piece(slot, kind):
            name, n = kind
            if name == "full":
                return buf.at[slot], gather_recv.at[base, 6, slot]
            if name == "half":
                start = pl.multiple_of(2 * quarter * n, 128)
                view = buf.at[slot, :, pl.ds(start, 2 * quarter)]
                return view, gather_recv.at[base, n, slot]
            view = buf.at[slot, :, pl.ds(pl.multiple_of(quarter * n, 128), quarter)]
            return view, gather_recv.at[base, 2 + n, slot]

        def send(slot, kind, mt, gt):
            view, recv = piece(slot, kind)
            copy = remote(view, view, gather_send.at[base, counter[0]], recv, mt, gt)
            copy.start()
            pending.append(copy)
            counter[0] += 1

        def arrived(slot, kind):
            view, recv = piece(slot, kind)
            remote(view, view, gather_send.at[base, 0], recv, m, g).wait_recv()

        full = ("full", 0)
        y_peer, core_peer, x_peer = at(a, other_b, c), at(a, b, other_c), g

        if split:
            mine, theirs = ("half", m), ("half", other_m)
            extra, rest_in = ("quarter", 2 * other_m), ("quarter", 2 * other_m + 1)
            rest_out = ("quarter", 2 * m + 1)

            def begin():
                for i in line:
                    send(g, mine, m, at(along(i), b, c))
                send(g, mine, m, y_peer)
                send(g, extra, m, y_peer)
                send(g, full, m, core_peer)

            def from_line(i):
                slot = at(along(i), b, c)
                arrived(slot, mine)
                send(slot, mine, other_m, x_peer)
                send(slot, mine, m, y_peer)
                send(slot, mine, m, core_peer)

            def from_x(i):
                slot = at(along(i), b, c)
                arrived(slot, theirs)
                send(slot, extra, m, y_peer)
                send(slot, theirs, m, core_peer)

            def from_y(i):
                slot = at(along(i), other_b, c)
                arrived(slot, mine)
                send(slot, rest_out, other_m, x_peer)
                send(slot, mine, m, core_peer)

            def from_y_extra(i):
                slot = at(along(i), other_b, c)
                arrived(slot, extra)
                send(slot, extra, m, core_peer)

            def from_x_rest(i):
                slot = at(along(i), other_b, c)
                arrived(slot, rest_in)
                send(slot, rest_in, m, core_peer)

            part = functools.partial
            steps = []
            for i in range(far):
                if i + 1 < far:
                    steps.append(part(from_line, i + 1))
                steps.append(part(from_y, i))
                if i + 1 < far:
                    steps.append(part(from_x, i + 1))
                steps.append(part(from_y_extra, i))
                steps.append(part(from_x_rest, i))

            def finish():
                for i in range(far):
                    slot = at(along(i), b, other_c)
                    if i == 0:
                        arrived(slot, full)
                    else:
                        arrived(slot, mine)
                        arrived(slot, theirs)
                    slot = at(along(i), other_b, other_c)
                    arrived(slot, mine)
                    arrived(slot, extra)
                    arrived(slot, rest_in)

            return begin, steps, finish

        def begin():
            for i in line:
                send(g, full, m, at(along(i), b, c))
            if near > 1:
                send(g, full, m, y_peer)
            if pair > 1:
                send(g, full, m, core_peer)

        def from_far(i):
            slot = at(along(i), b, c)
            arrived(slot, full)
            if near > 1:
                send(slot, full, m, y_peer)
            if pair > 1:
                send(slot, full, m, core_peer)

        def from_near(i):
            slot = at(along(i), other_b, c)
            arrived(slot, full)
            if pair > 1:
                send(slot, full, m, core_peer)

        steps = []
        for i in range(1, far):
            steps.append(functools.partial(from_far, i))
            if near > 1:
                steps.append(functools.partial(from_near, i - 1))
        if near > 1:
            steps.append(functools.partial(from_near, far - 1))

        def finish():
            if pair > 1:
                for i in range(far):
                    arrived(at(along(i), b, other_c), full)
                    if near > 1:
                        arrived(at(along(i), other_b, other_c), full)

        return begin, steps, finish

    split = members == 2 and near == 2 and pair == 2
    begin_qkv, steps_qkv, finish_qkv = gather(qkv_all, 0, split)
    begin_wo, steps_wo, finish_wo = gather(wo_all, 1, split)
    begin_wh, steps_wh, finish_wh = gather(wh_all, 2, False)

    begin_qkv()

    for load in loads[3:]:
        load.wait()
    x = states[0].astype(F32)
    center = x - jnp.mean(x, axis=-1, keepdims=True)
    inverse = lax.rsqrt(jnp.mean(center * center, axis=-1, keepdims=True) + epsilon)
    centred[...] = center * inverse
    normed[...] = (centred[...] * gain[...]).astype(BF)

    local = nb[...].T - (g * points - HALO)
    column = lax.broadcasted_iota(jnp.int32, (points, extent), 1)
    count = jnp.zeros((points, extent), F32)
    for k in range(nb.shape[0]):
        count = count + (local[:, k : k + 1] == column).astype(F32)
    count2 = jnp.concatenate([count, count], axis=0)

    for step in steps_qkv:
        step()
    begin_wo()
    begin_wh()
    finish_qkv()
    steps_out = []
    for n, step in enumerate(steps_wo):
        steps_out.append(step)
        if n % 2 == 1:
            steps_out += steps_wh[n // 2 : n // 2 + 1]
    steps_out += steps_wh[len(steps_wo) // 2 :]

    kv = dot(normed[...], qkv_all[:, :, inner : 3 * inner].reshape(width, 2 * inner))
    ext[HALO : HALO + points, :] = kv.astype(BF)
    up = remote(
        ext.at[pl.ds(points, HALO)],
        ext.at[pl.ds(0, HALO)],
        halo_send.at[0],
        halo_recv.at[0],
        m,
        after,
    )
    down = remote(
        ext.at[pl.ds(HALO, HALO)],
        ext.at[pl.ds(points + HALO, HALO)],
        halo_send.at[1],
        halo_recv.at[1],
        m,
        before,
    )
    up.start()
    down.start()
    query[...] = dot(
        normed[...], qkv_all[:, :, 0:inner].reshape(width, inner)
    ).astype(BF)
    up.wait()
    down.wait()

    lanes = 2 * head_dim
    first = lax.broadcasted_iota(jnp.int32, (points, lanes), 1) < head_dim
    scale = 1.0 / math.sqrt(head_dim)

    def stacked(rows):
        zero = jnp.zeros_like(rows)
        return jnp.concatenate(
            [jnp.where(first, rows, zero), jnp.where(first, zero, rows)], axis=0
        )

    def merged(rows):
        return jnp.where(first, rows[:points], rows[points:])

    couples = HEADS // 2
    per = -(-len(steps_out) // couples)
    for p in range(couples):
        cols = slice(p * lanes, (p + 1) * lanes)
        vcols = slice(inner + p * lanes, inner + (p + 1) * lanes)
        q2 = stacked(query[:, cols])
        score = dot(q2, ext[:, cols], 1, 1) * scale
        score = jnp.where(count2 > 0, score, -1e30)
        highest = jnp.max(score, axis=-1, keepdims=True)
        e = jnp.exp(score - highest)
        attention = e / jnp.sum(e * count2, axis=-1, keepdims=True)
        att[p] = attention
        weight = (attention.astype(BF).astype(F32) * count2).astype(BF)
        prob[p] = weight
        mixed[:, cols] = merged(dot(weight, ext[:, vcols])).astype(BF)
        for step in steps_out[p * per : (p + 1) * per]:
            step()
    finish_wo()
    finish_wh()

    out_full = wo_all[...].reshape(inner, width)
    head_full = wh_all[...].reshape(width, variables)
    layer_out[...] = (states[0].astype(F32) + dot(mixed[...], out_full)).astype(BF)
    forecasts[m] = dot(layer_out[...], head_full)
    fore = []
    for i in range(1, members):
        copy = remote(
            forecasts.at[m],
            forecasts.at[m],
            fore_send.at[i],
            fore_recv.at[m],
            lax.rem(m + i, members),
            g,
        )
        copy.start()
        fore.append(copy)
    mine = forecasts[m]
    slope = gradient_of(mine - obs[...])
    for i in range(1, members):
        j = lax.rem(m + i, members)
        remote(
            forecasts.at[j], forecasts.at[j], fore_send.at[i], fore_recv.at[j], m, g
        ).wait_recv()
        slope = slope - gradient_of(mine - forecasts[j]) / (members - 1)
    grad_fore = slope.astype(BF)

    rows_head, rows_mix = wh.shape[0], wo.shape[0]
    head_part = (
        dot(layer_out[...], grad_fore, 0, 0)
        .astype(BF)
        .reshape(quads, pair, rows_head, variables)
    )
    mix_part = (
        dot(mixed[...], grad_fore, 0, 0)
        .astype(BF)
        .reshape(quads, pair, rows_mix, variables)
    )
    for n in range(pair):
        stage[n, :, 0:rows_head, :] = head_part[:, n]
        stage[n, :, rows_head : rows_head + rows_mix, :] = mix_part[:, n]
    crossing = remote(
        stage.at[other_c],
        sibling,
        share_send.at[0],
        share_recv.at[quads],
        m,
        at(a, b, other_c),
    )
    if pair > 1:
        crossing.start()

    grad_out[...] = dot(grad_fore, head_full, 1, 1)
    grad_mixed[...] = dot(grad_out[...].astype(BF), out_full, 1, 1).astype(BF)

    if pair > 1:
        crossing.wait()
        stage_sum[...] = (stage[c].astype(F32) + sibling[...].astype(F32)).astype(BF)
    else:
        stage_sum[...] = stage[0]
    sharing = []
    for i in range(1, quads):
        t = lax.rem(quad + i, quads)
        copy = remote(
            stage_sum.at[t],
            shares.at[quad],
            share_send.at[i],
            share_recv.at[quad],
            m,
            t * pair + c,
        )
        copy.start()
        sharing.append(copy)

    for p in range(couples):
        cols = slice(p * lanes, (p + 1) * lanes)
        vcols = slice(inner + p * lanes, inner + (p + 1) * lanes)
        q2 = stacked(query[:, cols])
        g2 = stacked(grad_mixed[:, cols])
        attention = att[p]
        grad_prob = dot(g2, ext[:, vcols], 1, 1)
        weighted = attention * count2
        middle = jnp.sum(weighted * grad_prob, axis=-1, keepdims=True)
        grad_score = (weighted * (grad_prob - middle) * scale).astype(BF)
        grad_ext[:, cols] = dot(grad_score, q2, 0, 0)
        grad_ext[:, vcols] = dot(prob[p], g2, 0, 0)
        grad_query[:, cols] = merged(dot(grad_score, ext[:, cols])).astype(BF)

    halo_out[0] = grad_ext[0:HALO, :].astype(BF)
    halo_out[1] = grad_ext[points + HALO : points + 2 * HALO, :].astype(BF)
    back_down = remote(
        halo_out.at[0], halo_in.at[0], halo_send.at[2], halo_recv.at[2], m, before
    )
    back_up = remote(
        halo_out.at[1], halo_in.at[1], halo_send.at[3], halo_recv.at[3], m, after
    )
    back_down.start()
    back_up.start()
    grad_normed = dot(
        grad_query[...], qkv_all[:, :, 0:inner].reshape(width, inner), 1, 1
    )
    back_down.wait()
    back_up.wait()
    grad_kv[0] = grad_ext[HALO : HALO + points, :]
    grad_kv[0, 0:HALO, :] += halo_in[1].astype(F32)
    grad_kv[0, points - HALO : points, :] += halo_in[0].astype(F32)
    grad_normed = grad_normed + dot(
        grad_kv[0].astype(BF),
        qkv_all[:, :, inner : 3 * inner].reshape(width, 2 * inner),
        1,
        1,
    )
    total = stage_sum[quad].astype(F32)
    for i in range(1, quads):
        t = lax.rem(quad + quads - i, quads)
        remote(
            stage_sum.at[t], shares.at[t], share_send.at[i], share_recv.at[t], m, g
        ).wait_recv()
        total = total + shares[t].astype(F32)
    totals[m] = total.astype(BF)
    for i in range(1, members):
        copy = remote(
            totals.at[m],
            totals.at[m],
            total_send.at[i],
            total_recv.at[m],
            lax.rem(m + i, members),
            g,
        )
        copy.start()
        sharing.append(copy)
    gg = grad_normed * gain[...]
    cen = centred[...]
    grad_states = inverse * (
        gg
        - jnp.mean(gg, axis=-1, keepdims=True)
        - cen * jnp.mean(gg * cen, axis=-1, keepdims=True)
    )
    grad_input[0] = (grad_out[...] + grad_states).astype(BF)

    total = totals[m].astype(F32)
    for i in range(1, members):
        j = lax.rem(m + i, members)
        remote(
            totals.at[j], totals.at[j], total_send.at[i], total_recv.at[j], m, g
        ).wait_recv()
        total = total + totals[j].astype(F32)
    scaling = 1.0 / math.sqrt(members * grid * points)
    grad_head[...] = total[0:rows_head] * scaling
    grad_mixing[...] = (
        dot(total[rows_head : rows_head + rows_mix].astype(BF), head_full, 1, 1)
        * scaling
    )

    for copy in pending + fore + sharing:
        copy.wait_send()


def solution(mesh):
    members, grid = mesh.shape["member"], mesh.shape["grid"]
    far, near, pair = factors(grid)

    def shards(states, gain, wq, wk, wv, wo, wh, nb, obs):
        points, width = states.shape[1], states.shape[2]
        inner = wq.shape[1]
        variables = obs.shape[1]
        extent = points + 2 * HALO
        quads = grid // pair
        slab = wh.shape[0] + wo.shape[0]
        sends = 4 * grid
        vm = pltpu.VMEM
        dma = pltpu.SemaphoreType.DMA
        couples = HEADS // 2
        return pl.pallas_call(
            functools.partial(kernel, members, grid),
            out_shape=(
                jax.ShapeDtypeStruct((1, points, width), BF),
                jax.ShapeDtypeStruct(wo.shape, F32),
                jax.ShapeDtypeStruct(wh.shape, F32),
                jax.ShapeDtypeStruct((1, points, 2 * inner), F32),
            ),
            in_specs=[pl.BlockSpec(memory_space=pl.ANY)] * 9,
            out_specs=(pl.BlockSpec(memory_space=pltpu.VMEM),) * 4,
            scratch_shapes=[
                vm(states.shape, BF),
                vm((1, width), F32),
                vm((nb.shape[1], nb.shape[0]), jnp.int32),
                vm(obs.shape, F32),
                vm((grid, wq.shape[0], 3 * inner), BF),
                vm((grid,) + wo.shape, BF),
                vm((grid,) + wh.shape, BF),
                vm((points, width), F32),
                vm((points, width), BF),
                vm((points, inner), BF),
                vm((extent, 2 * inner), BF),
                vm((couples, 2 * points, extent), F32),
                vm((couples, 2 * points, extent), BF),
                vm((points, inner), BF),
                vm((points, width), BF),
                vm((members, points, variables), F32),
                vm((points, width), F32),
                vm((points, inner), BF),
                vm((points, inner), BF),
                vm((extent, 2 * inner), F32),
                vm((2, HALO, 2 * inner), BF),
                vm((2, HALO, 2 * inner), BF),
                vm((pair, quads, slab, variables), BF),
                vm((quads, slab, variables), BF),
                vm((quads, slab, variables), BF),
                vm((quads, slab, variables), BF),
                vm((members, slab, variables), BF),
                dma((9,)),
                dma((3, sends)),
                dma((3, 7, grid)),
                dma((4,)),
                dma((4,)),
                dma((members,)),
                dma((members,)),
                dma((quads,)),
                dma((quads + 1,)),
                dma((members,)),
                dma((members,)),
            ],
            compiler_params=pltpu.CompilerParams(
                collective_id=0,
                has_side_effects=True,
                vmem_limit_bytes=44 * 1024 * 1024,
            ),
        )(states, gain.reshape(1, width), wq, wk, wv, wo, wh, nb.T, obs)

    return jax.shard_map(
        shards,
        mesh=mesh,
        in_specs=(
            P("member", "grid", None),
            P(),
            P("grid", None),
            P("grid", None),
            P("grid", None),
            P("grid", None),
            P("grid", None),
            P("grid", None),
            P("grid", None),
        ),
        out_specs=(
            P("member", "grid", None),
            P("grid", None),
            P("grid", None),
            P("member", "grid", None),
        ),
        check_vma=False,
    )
```

```python
import functools
import math

import jax
import jax.numpy as jnp
from jax import lax
from jax.experimental import pallas as pl
from jax.experimental.pallas import tpu as pltpu
from jax.sharding import PartitionSpec as P

HEADS = 8
HALO = 32
MESH = pl.DeviceIdType.MESH

epsilon = 1e-05
smooth = 0.1

BF = jnp.bfloat16
F32 = jnp.float32


def dot(left, right, left_dim=1, right_dim=0):
    return lax.dot_general(
        left,
        right,
        (((left_dim,), (right_dim,)), ((), ())),
        preferred_element_type=F32,
    )


def gradient_of(spread):
    return spread * lax.rsqrt(spread * spread + smooth * smooth)


def factors(total):
    pair = 2 if total % 2 == 0 else 1
    near = 2 if (total // pair) % 2 == 0 else 1
    return total // (pair * near), near, pair


def kernel(
    members,
    grid,
    states_hbm,
    gain_hbm,
    wq,
    wk,
    wv,
    wo,
    wh,
    nb_hbm,
    obs_hbm,
    grad_input,
    grad_mixing,
    grad_head,
    grad_kv,
    states,
    gain,
    nb,
    obs,
    qkv_all,
    wo_all,
    wh_all,
    centred,
    normed,
    query,
    ext,
    att,
    prob,
    mixed,
    layer_out,
    forecasts,
    grad_out,
    grad_mixed,
    grad_query,
    grad_ext,
    halo_out,
    halo_in,
    stage,
    sibling,
    stage_sum,
    shares,
    totals,
    load_sem,
    gather_send,
    gather_recv,
    halo_send,
    halo_recv,
    fore_send,
    fore_recv,
    share_send,
    share_recv,
    total_send,
    total_recv,
):
    m = lax.axis_index("member")
    g = lax.axis_index("grid")
    points, width = states.shape[1], states.shape[2]
    inner = wq.shape[1]
    extent = points + 2 * HALO
    variables = obs.shape[1]
    head_dim = inner // HEADS
    far, near, pair = factors(grid)
    a, b, c = g // (near * pair), (g // pair) % near, g % pair
    quads, quad = grid // pair, g // pair
    after, before = lax.rem(g + 1, grid), lax.rem(g + grid - 1, grid)

    def remote(src, dst, send, recv, mt, gt):
        return pltpu.make_async_remote_copy(
            src_ref=src,
            dst_ref=dst,
            send_sem=send,
            recv_sem=recv,
            device_id={"member": mt, "grid": gt},
            device_id_type=MESH,
        )

    loads = [
        pltpu.make_async_copy(src, dst, load_sem.at[n])
        for n, (src, dst) in enumerate(
            [
                (wq, qkv_all.at[g, :, pl.ds(0, inner)]),
                (wk, qkv_all.at[g, :, pl.ds(inner, inner)]),
                (wv, qkv_all.at[g, :, pl.ds(2 * inner, inner)]),
                (states_hbm, states),
                (gain_hbm, gain),
                (nb_hbm, nb),
                (wo, wo_all.at[g]),
                (wh, wh_all.at[g]),
                (obs_hbm, obs),
            ]
        )
    ]
    for load in loads:
        load.start()

    barrier = pltpu.get_barrier_semaphore()
    peers = [(m, after), (m, before)]
    peers += [(m, lax.rem(quad + i, quads) * pair + c) for i in range(1, quads)]
    peers += [(m, quad * pair + lax.rem(c + i, pair)) for i in range(1, pair)]
    peers += [(lax.rem(m + i, members), g) for i in range(1, members)]
    for mt, gt in peers:
        pl.semaphore_signal(
            barrier, inc=1, device_id={"member": mt, "grid": gt}, device_id_type=MESH
        )
    for load in loads[:3]:
        load.wait()
    pl.semaphore_wait(barrier, len(peers))

    pending = []

    def at(ai, bi, ci):
        return (ai * near + bi) * pair + ci

    def along(i):
        if i == 0:
            return a
        if far != 4:
            return lax.rem(a + i, far)
        if i == 1:
            return a + 1 - 2 * lax.rem(a, 2)
        if i == 2:
            return lax.rem(a + 2, 4)
        return 3 - a

    other_m, other_b, other_c = 1 - m, lax.rem(b + 1, near), lax.rem(c + 1, pair)
    line = [2, 1, 3] if far == 4 else list(range(1, far))

    def gather(buf, base, split):
        counter = [0]
        quarter = buf.shape[2] // 4

        def piece(slot, kind):
            name, n = kind
            if name == "full":
                return buf.at[slot], gather_recv.at[base, 6, slot]
            if name == "half":
                start = pl.multiple_of(2 * quarter * n, 128)
                view = buf.at[slot, :, pl.ds(start, 2 * quarter)]
                return view, gather_recv.at[base, n, slot]
            view = buf.at[slot, :, pl.ds(pl.multiple_of(quarter * n, 128), quarter)]
            return view, gather_recv.at[base, 2 + n, slot]

        def send(slot, kind, mt, gt):
            view, recv = piece(slot, kind)
            copy = remote(view, view, gather_send.at[base, counter[0]], recv, mt, gt)
            copy.start()
            pending.append(copy)
            counter[0] += 1

        def arrived(slot, kind):
            view, recv = piece(slot, kind)
            remote(view, view, gather_send.at[base, 0], recv, m, g).wait_recv()

        full = ("full", 0)
        y_peer, core_peer, x_peer = at(a, other_b, c), at(a, b, other_c), g

        if split:
            mine, theirs = ("half", m), ("half", other_m)
            extra, rest_in = ("quarter", 2 * other_m), ("quarter", 2 * other_m + 1)
            rest_out = ("quarter", 2 * m + 1)

            def begin():
                for i in line:
                    send(g, mine, m, at(along(i), b, c))
                send(g, mine, m, y_peer)
                send(g, extra, m, y_peer)
                send(g, full, m, core_peer)

            def from_line(i):
                slot = at(along(i), b, c)
                arrived(slot, mine)
                send(slot, mine, other_m, x_peer)
                send(slot, mine, m, y_peer)
                send(slot, mine, m, core_peer)

            def from_x(i):
                slot = at(along(i), b, c)
                arrived(slot, theirs)
                send(slot, extra, m, y_peer)
                send(slot, theirs, m, core_peer)

            def from_y(i):
                slot = at(along(i), other_b, c)
                arrived(slot, mine)
                send(slot, rest_out, other_m, x_peer)
                send(slot, mine, m, core_peer)

            def from_y_extra(i):
                slot = at(along(i), other_b, c)
                arrived(slot, extra)
                send(slot, extra, m, core_peer)

            def from_x_rest(i):
                slot = at(along(i), other_b, c)
                arrived(slot, rest_in)
                send(slot, rest_in, m, core_peer)

            part = functools.partial
            steps = []
            for i in range(far):
                if i + 1 < far:
                    steps.append(part(from_line, i + 1))
                steps.append(part(from_y, i))
                if i + 1 < far:
                    steps.append(part(from_x, i + 1))
                steps.append(part(from_y_extra, i))
                steps.append(part(from_x_rest, i))

            def finish():
                for i in range(far):
                    slot = at(along(i), b, other_c)
                    if i == 0:
                        arrived(slot, full)
                    else:
                        arrived(slot, mine)
                        arrived(slot, theirs)
                    slot = at(along(i), other_b, other_c)
                    arrived(slot, mine)
                    arrived(slot, extra)
                    arrived(slot, rest_in)

            return begin, steps, finish

        def begin():
            for i in line:
                send(g, full, m, at(along(i), b, c))
            if near > 1:
                send(g, full, m, y_peer)
            if pair > 1:
                send(g, full, m, core_peer)

        def from_far(i):
            slot = at(along(i), b, c)
            arrived(slot, full)
            if near > 1:
                send(slot, full, m, y_peer)
            if pair > 1:
                send(slot, full, m, core_peer)

        def from_near(i):
            slot = at(along(i), other_b, c)
            arrived(slot, full)
            if pair > 1:
                send(slot, full, m, core_peer)

        steps = []
        for i in range(1, far):
            steps.append(functools.partial(from_far, i))
            if near > 1:
                steps.append(functools.partial(from_near, i - 1))
        if near > 1:
            steps.append(functools.partial(from_near, far - 1))

        def finish():
            if pair > 1:
                for i in range(far):
                    arrived(at(along(i), b, other_c), full)
                    if near > 1:
                        arrived(at(along(i), other_b, other_c), full)

        return begin, steps, finish

    split = members == 2 and near == 2 and pair == 2
    begin_qkv, steps_qkv, finish_qkv = gather(qkv_all, 0, split)
    begin_wo, steps_wo, finish_wo = gather(wo_all, 1, False)
    begin_wh, steps_wh, finish_wh = gather(wh_all, 2, False)

    begin_qkv()

    for load in loads[3:]:
        load.wait()
    x = states[0].astype(F32)
    center = x - jnp.mean(x, axis=-1, keepdims=True)
    inverse = lax.rsqrt(jnp.mean(center * center, axis=-1, keepdims=True) + epsilon)
    centred[...] = center * inverse
    normed[...] = (centred[...] * gain[...]).astype(BF)

    local = nb[...].T - (g * points - HALO)
    column = lax.broadcasted_iota(jnp.int32, (points, extent), 1)
    count = jnp.zeros((points, extent), F32)
    for k in range(nb.shape[0]):
        count = count + (local[:, k : k + 1] == column).astype(F32)
    count2 = jnp.concatenate([count, count], axis=0)

    for n, step in enumerate(steps_qkv):
        step()
        if n == len(steps_qkv) // 3:
            begin_wo()
            begin_wh()
    finish_qkv()
    steps_out = []
    for n, step in enumerate(steps_wo):
        steps_out.append(step)
        if n % 2 == 1:
            steps_out += steps_wh[n // 2 : n // 2 + 1]
    steps_out += steps_wh[len(steps_wo) // 2 :]

    kv = dot(normed[...], qkv_all[:, :, inner : 3 * inner].reshape(width, 2 * inner))
    ext[HALO : HALO + points, :] = kv.astype(BF)
    up = remote(
        ext.at[pl.ds(points, HALO)],
        ext.at[pl.ds(0, HALO)],
        halo_send.at[0],
        halo_recv.at[0],
        m,
        after,
    )
    down = remote(
        ext.at[pl.ds(HALO, HALO)],
        ext.at[pl.ds(points + HALO, HALO)],
        halo_send.at[1],
        halo_recv.at[1],
        m,
        before,
    )
    up.start()
    down.start()
    query[...] = dot(
        normed[...], qkv_all[:, :, 0:inner].reshape(width, inner)
    ).astype(BF)
    up.wait()
    down.wait()

    lanes = 2 * head_dim
    first = lax.broadcasted_iota(jnp.int32, (points, lanes), 1) < head_dim
    scale = 1.0 / math.sqrt(head_dim)

    def stacked(rows):
        zero = jnp.zeros_like(rows)
        return jnp.concatenate(
            [jnp.where(first, rows, zero), jnp.where(first, zero, rows)], axis=0
        )

    def merged(rows):
        return jnp.where(first, rows[:points], rows[points:])

    couples = HEADS // 2
    per = -(-len(steps_out) // couples)
    for p in range(couples):
        cols = slice(p * lanes, (p + 1) * lanes)
        vcols = slice(inner + p * lanes, inner + (p + 1) * lanes)
        q2 = stacked(query[:, cols])
        score = dot(q2, ext[:, cols], 1, 1) * scale
        score = jnp.where(count2 > 0, score, -1e30)
        highest = jnp.max(score, axis=-1, keepdims=True)
        e = jnp.exp(score - highest)
        attention = e / jnp.sum(e * count2, axis=-1, keepdims=True)
        att[p] = attention
        weight = (attention.astype(BF).astype(F32) * count2).astype(BF)
        prob[p] = weight
        mixed[:, cols] = merged(dot(weight, ext[:, vcols])).astype(BF)
        for step in steps_out[p * per : (p + 1) * per]:
            step()
    finish_wo()
    finish_wh()

    out_full = wo_all[...].reshape(inner, width)
    head_full = wh_all[...].reshape(width, variables)
    layer_out[...] = (states[0].astype(F32) + dot(mixed[...], out_full)).astype(BF)
    forecasts[m] = dot(layer_out[...], head_full)
    fore = []
    for i in range(1, members):
        copy = remote(
            forecasts.at[m],
            forecasts.at[m],
            fore_send.at[i],
            fore_recv.at[m],
            lax.rem(m + i, members),
            g,
        )
        copy.start()
        fore.append(copy)
    mine = forecasts[m]
    slope = gradient_of(mine - obs[...])
    for i in range(1, members):
        j = lax.rem(m + i, members)
        remote(
            forecasts.at[j], forecasts.at[j], fore_send.at[i], fore_recv.at[j], m, g
        ).wait_recv()
        slope = slope - gradient_of(mine - forecasts[j]) / (members - 1)
    grad_fore = slope.astype(BF)

    rows_head, rows_mix = wh.shape[0], wo.shape[0]
    head_part = (
        dot(layer_out[...], grad_fore, 0, 0)
        .astype(BF)
        .reshape(quads, pair, rows_head, variables)
    )
    mix_part = (
        dot(mixed[...], grad_fore, 0, 0)
        .astype(BF)
        .reshape(quads, pair, rows_mix, variables)
    )
    for n in range(pair):
        stage[n, :, 0:rows_head, :] = head_part[:, n]
        stage[n, :, rows_head : rows_head + rows_mix, :] = mix_part[:, n]
    crossing = remote(
        stage.at[other_c],
        sibling,
        share_send.at[0],
        share_recv.at[quads],
        m,
        at(a, b, other_c),
    )
    if pair > 1:
        crossing.start()

    grad_out[...] = dot(grad_fore, head_full, 1, 1)
    grad_mixed[...] = dot(grad_out[...].astype(BF), out_full, 1, 1).astype(BF)

    if pair > 1:
        crossing.wait()
        stage_sum[...] = (stage[c].astype(F32) + sibling[...].astype(F32)).astype(BF)
    else:
        stage_sum[...] = stage[0]
    sharing = []
    for i in range(1, quads):
        t = lax.rem(quad + i, quads)
        copy = remote(
            stage_sum.at[t],
            shares.at[quad],
            share_send.at[i],
            share_recv.at[quad],
            m,
            t * pair + c,
        )
        copy.start()
        sharing.append(copy)

    for p in range(couples):
        cols = slice(p * lanes, (p + 1) * lanes)
        vcols = slice(inner + p * lanes, inner + (p + 1) * lanes)
        q2 = stacked(query[:, cols])
        g2 = stacked(grad_mixed[:, cols])
        attention = att[p]
        grad_prob = dot(g2, ext[:, vcols], 1, 1)
        weighted = attention * count2
        middle = jnp.sum(weighted * grad_prob, axis=-1, keepdims=True)
        grad_score = (weighted * (grad_prob - middle) * scale).astype(BF)
        grad_ext[:, cols] = dot(grad_score, q2, 0, 0)
        grad_ext[:, vcols] = dot(prob[p], g2, 0, 0)
        grad_query[:, cols] = merged(dot(grad_score, ext[:, cols])).astype(BF)

    halo_out[0] = grad_ext[0:HALO, :].astype(BF)
    halo_out[1] = grad_ext[points + HALO : points + 2 * HALO, :].astype(BF)
    back_down = remote(
        halo_out.at[0], halo_in.at[0], halo_send.at[2], halo_recv.at[2], m, before
    )
    back_up = remote(
        halo_out.at[1], halo_in.at[1], halo_send.at[3], halo_recv.at[3], m, after
    )
    back_down.start()
    back_up.start()
    grad_normed = dot(
        grad_query[...], qkv_all[:, :, 0:inner].reshape(width, inner), 1, 1
    )
    back_down.wait()
    back_up.wait()
    grad_kv[0] = grad_ext[HALO : HALO + points, :]
    grad_kv[0, 0:HALO, :] += halo_in[1].astype(F32)
    grad_kv[0, points - HALO : points, :] += halo_in[0].astype(F32)
    grad_normed = grad_normed + dot(
        grad_kv[0].astype(BF),
        qkv_all[:, :, inner : 3 * inner].reshape(width, 2 * inner),
        1,
        1,
    )
    total = stage_sum[quad].astype(F32)
    for i in range(1, quads):
        t = lax.rem(quad + quads - i, quads)
        remote(
            stage_sum.at[t], shares.at[t], share_send.at[i], share_recv.at[t], m, g
        ).wait_recv()
        total = total + shares[t].astype(F32)
    totals[m] = total.astype(BF)
    for i in range(1, members):
        copy = remote(
            totals.at[m],
            totals.at[m],
            total_send.at[i],
            total_recv.at[m],
            lax.rem(m + i, members),
            g,
        )
        copy.start()
        sharing.append(copy)
    gg = grad_normed * gain[...]
    cen = centred[...]
    grad_states = inverse * (
        gg
        - jnp.mean(gg, axis=-1, keepdims=True)
        - cen * jnp.mean(gg * cen, axis=-1, keepdims=True)
    )
    grad_input[0] = (grad_out[...] + grad_states).astype(BF)

    total = totals[m].astype(F32)
    for i in range(1, members):
        j = lax.rem(m + i, members)
        remote(
            totals.at[j], totals.at[j], total_send.at[i], total_recv.at[j], m, g
        ).wait_recv()
        total = total + totals[j].astype(F32)
    scaling = 1.0 / math.sqrt(members * grid * points)
    grad_head[...] = total[0:rows_head] * scaling
    grad_mixing[...] = (
        dot(total[rows_head : rows_head + rows_mix].astype(BF), head_full, 1, 1)
        * scaling
    )

    for copy in pending + fore + sharing:
        copy.wait_send()


def solution(mesh):
    members, grid = mesh.shape["member"], mesh.shape["grid"]
    far, near, pair = factors(grid)

    def shards(states, gain, wq, wk, wv, wo, wh, nb, obs):
        points, width = states.shape[1], states.shape[2]
        inner = wq.shape[1]
        variables = obs.shape[1]
        extent = points + 2 * HALO
        quads = grid // pair
        slab = wh.shape[0] + wo.shape[0]
        sends = 4 * grid
        vm = pltpu.VMEM
        dma = pltpu.SemaphoreType.DMA
        couples = HEADS // 2
        return pl.pallas_call(
            functools.partial(kernel, members, grid),
            out_shape=(
                jax.ShapeDtypeStruct((1, points, width), BF),
                jax.ShapeDtypeStruct(wo.shape, F32),
                jax.ShapeDtypeStruct(wh.shape, F32),
                jax.ShapeDtypeStruct((1, points, 2 * inner), F32),
            ),
            in_specs=[pl.BlockSpec(memory_space=pltpu.HBM)] * 9,
            out_specs=(pl.BlockSpec(memory_space=pltpu.VMEM),) * 4,
            scratch_shapes=[
                vm(states.shape, BF),
                vm((1, width), F32),
                vm((nb.shape[1], nb.shape[0]), jnp.int32),
                vm(obs.shape, F32),
                vm((grid, wq.shape[0], 3 * inner), BF),
                vm((grid,) + wo.shape, BF),
                vm((grid,) + wh.shape, BF),
                vm((points, width), F32),
                vm((points, width), BF),
                vm((points, inner), BF),
                vm((extent, 2 * inner), BF),
                vm((couples, 2 * points, extent), F32),
                vm((couples, 2 * points, extent), BF),
                vm((points, inner), BF),
                vm((points, width), BF),
                vm((members, points, variables), F32),
                vm((points, width), F32),
                vm((points, inner), BF),
                vm((points, inner), BF),
                vm((extent, 2 * inner), F32),
                vm((2, HALO, 2 * inner), BF),
                vm((2, HALO, 2 * inner), BF),
                vm((pair, quads, slab, variables), BF),
                vm((quads, slab, variables), BF),
                vm((quads, slab, variables), BF),
                vm((quads, slab, variables), BF),
                vm((members, slab, variables), BF),
                dma((9,)),
                dma((3, sends)),
                dma((3, 7, grid)),
                dma((4,)),
                dma((4,)),
                dma((members,)),
                dma((members,)),
                dma((quads,)),
                dma((quads + 1,)),
                dma((members,)),
                dma((members,)),
            ],
            compiler_params=pltpu.CompilerParams(
                collective_id=0,
                has_side_effects=True,
                vmem_limit_bytes=44 * 1024 * 1024,
            ),
        )(states, gain.reshape(1, width), wq, wk, wv, wo, wh, nb.T, obs)

    return jax.shard_map(
        shards,
        mesh=mesh,
        in_specs=(
            P("member", "grid", None),
            P(),
            P("grid", None),
            P("grid", None),
            P("grid", None),
            P("grid", None),
            P("grid", None),
            P("grid", None),
            P("grid", None),
        ),
        out_specs=(
            P("member", "grid", None),
            P("grid", None),
            P("grid", None),
            P("member", "grid", None),
        ),
        check_vma=False,
    )
```
